32 devices in a mesh: groups: 2 (over y), cand: 4 (over x, core), hist: 4 (over z).
Axes of the slice: x: 2, y: 2, z: 4, core: 2. Of those that a mesh axis runs over, the one named last changes fastest.
Arguments:
- cand_feats: bfloat16 [2048, 256], P(('groups', 'cand')), parts along dimension 0, may hold values from -6 to 6
- cat_table: bfloat16 [4, 256], P('groups'), parts along dimension 0, may hold values from -5 to 5
- cand_cat: int32 [2048], P(('groups', 'cand')), parts along dimension 0, may hold values from 0 to 1
- cand_blocks: int32 [2048, 16], P(('groups', 'cand')), parts along dimension 0, may hold values from 0 to 127, as said below
- cand_count: int32 [2048], P(('groups', 'cand')), parts along dimension 0, may hold values from 1 to 16
- keys: bfloat16 [32768, 256], P(('groups', 'cand', 'hist')), parts along dimension 0, may hold values from -6 to 6
- values: bfloat16 [32768, 256], P(('groups', 'cand', 'hist')), parts along dimension 0, may hold values from -6 to 6
- w_query: bfloat16 [256, 256], replicated, may hold values from -0.375 to 0.375
- norm_gain: float32 [256], replicated, may hold values from 0.25 to 1.75
- w_up: bfloat16 [256, 1024], replicated, may hold values from -0.375 to 0.375
- w_down: bfloat16 [1024, 256], replicated, may hold values from -0.1875 to 0.1875
Outputs:
- ranked: bfloat16 [2048, 256], P(('groups', 'cand')), parts along dimension 0
The draws below stay inside these ranges and needn't reach their ends.
There are 2 independent parts, one for each index of `groups`. The reference program is written for one: setup_inputs(seed, part) draws one part's arguments, and reference() takes and returns one part's arrays. A program takes and returns all parts, laid end to end along the dimension named above; an argument that names none is the same for every part. Nothing has to cross between parts.
Inputs may be any that keep to these rules, and one draw needn't show every extreme that they name: `cand_blocks`: block b has category b % 2; every block a candidate lists has the candidate's category, and the 16 ids in one row are distinct. Some candidate uses all 16 slots and some only one.
All inputs are finite; a program needn't handle non-finite values.
Results may differ from the reference program's by a relative error of at most 0.0055.
Values may be sent and summed in bfloat16 or wider, within the bound.
A program may use at most 64 MiB of HBM per device.

```python
import math
import jax
import jax.numpy as jnp
from jax import lax

D = 256
HEADS = 4
HEAD_DIM = 64
FFN = 1024
BLOCK = 128
LIST = 16
CATS = 2
CANDS = 1024
NB = 128
BEHAV = 16384
CAT_BLOCKS = 64


def category_draw(key):
    return jax.random.randint(jax.random.fold_in(key, 11), (CANDS,), 0, CATS, dtype=jnp.int32)


def draw_cand_cat(key, part):
    return category_draw(key)


def draw_cand_blocks(key, part):
    category = category_draw(key)
    ranks = jax.random.randint(jax.random.fold_in(key, 15), (CANDS, CAT_BLOCKS), 0, 4096, dtype=jnp.int32)
    scores = ranks * CAT_BLOCKS + jnp.arange(CAT_BLOCKS, dtype=jnp.int32)[None, :]
    within = lax.top_k(scores, LIST)[1].astype(jnp.int32)
    return (category[:, None] + CATS * within).astype(jnp.int32)


def draw_cand_count(key, part):
    counts = jax.random.randint(jax.random.fold_in(key, 14), (CANDS,), 1, LIST + 1, dtype=jnp.int32)
    position = jnp.arange(CANDS, dtype=jnp.int32)
    counts = jnp.where(position % 64 == 0, LIST, counts)
    counts = jnp.where(position % 64 == 1, 1, counts)
    return counts.astype(jnp.int32)


def steps_of(own_key, shape, cuts, low, largest):
    level, own = 1.0, jax.random.fold_in(own_key, 6)
    for dim, parts in cuts:
        draws = jnp.exp(jax.random.uniform(jax.random.fold_in(own, dim), (parts,), jnp.float32, low / len(cuts), largest / len(cuts)))
        level = level * jnp.repeat(draws, shape[dim] // parts).reshape([-1 if axis == dim else 1 for axis in range(len(shape))])
    return level


def noise(key, extent, scale, reach, split=(), kind=jnp.bfloat16):
    values = scale * jax.random.normal(key, extent, jnp.float32)
    if split:
        values = values * steps_of(key, extent, split, -0.22, 0.18)
    return jnp.clip(values, -reach, reach).astype(kind)


def setup_inputs(seed: int = 0, part: int = 0) -> dict:
    seeds = jax.random.split(jax.random.key(seed), 12)
    part_keys = jax.random.split(jax.random.fold_in(seeds[11], part), 12)
    return {
        "cand_feats": noise(part_keys[0], (CANDS, D), 1.0, 6.0, ((0, 4),)),
        "cat_table": noise(part_keys[1], (CATS, D), 0.7, 5.0),
        "cand_cat": draw_cand_cat(jax.random.fold_in(jax.random.fold_in(seeds[11], part), 71), part),
        "cand_blocks": draw_cand_blocks(jax.random.fold_in(jax.random.fold_in(seeds[11], part), 71), part),
        "cand_count": draw_cand_count(jax.random.fold_in(jax.random.fold_in(seeds[11], part), 71), part),
        "keys": noise(part_keys[5], (BEHAV, D), 1.0, 6.0, ((0, 16),)),
        "values": noise(part_keys[6], (BEHAV, D), 1.0, 6.0, ((0, 16),)),
        "w_query": noise(seeds[7], (D, D), D ** -0.5, 0.375),
        "norm_gain": jnp.clip(1.0 + 0.15 * jax.random.normal(seeds[8], (D,), jnp.float32), 0.25, 1.75),
        "w_up": noise(seeds[9], (D, FFN), D ** -0.5, 0.375),
        "w_down": noise(seeds[10], (FFN, D), FFN ** -0.5, 0.1875),
    }


def reference(cand_feats, cat_table, cand_cat, cand_blocks, cand_count, keys, values, w_query, norm_gain, w_up, w_down):
    onehot = (cand_cat[:, None] == jnp.arange(CATS, dtype=jnp.int32)[None, :]).astype(jnp.bfloat16)
    embedded = jnp.dot(onehot, cat_table, preferred_element_type=jnp.float32)
    query_input = (cand_feats.astype(jnp.float32) + embedded).astype(jnp.bfloat16)
    query = jnp.dot(query_input, w_query, preferred_element_type=jnp.float32).astype(jnp.bfloat16)
    query = query.reshape(CANDS, HEADS, HEAD_DIM)
    key_blocks = keys.reshape(NB, BLOCK, HEADS, HEAD_DIM)
    value_blocks = values.reshape(NB, BLOCK, HEADS, HEAD_DIM)
    score_scale = 1.0 / math.sqrt(HEAD_DIM)
    row_block = math.gcd(CANDS, 64)

    def attend(inputs_block):
        query_rows, block_ids, counts = inputs_block
        key_rows = key_blocks[block_ids].astype(jnp.float32)
        value_rows = value_blocks[block_ids].astype(jnp.float32)
        scores = jnp.einsum('rhd,rlbhd->rlbh', query_rows.astype(jnp.float32), key_rows) * score_scale
        slot_live = (jnp.arange(LIST, dtype=jnp.int32)[None, :] < counts[:, None]).astype(jnp.float32)
        weights_bf = (jax.nn.silu(scores) * slot_live[:, :, None, None]).astype(jnp.bfloat16)
        return jnp.einsum('rlbh,rlbhd->rhd', weights_bf.astype(jnp.float32), value_rows)
    attended = lax.map(attend, (query.reshape(-1, row_block, HEADS, HEAD_DIM), cand_blocks.reshape(-1, row_block, LIST), cand_count.reshape(-1, row_block)))
    attended = attended.reshape(CANDS, D)
    mean_square = lax.optimization_barrier(jnp.mean(attended * attended, axis=-1, keepdims=True))
    normed = (attended * lax.rsqrt(mean_square + 1e-06) * norm_gain).astype(jnp.bfloat16)
    hidden = jax.nn.silu(jnp.dot(normed, w_up, preferred_element_type=jnp.float32)).astype(jnp.bfloat16)
    result = cand_feats.astype(jnp.float32) + jnp.dot(hidden, w_down, preferred_element_type=jnp.float32)
    return result.astype(jnp.bfloat16)
```

```python
import functools
import math

import jax
import jax.numpy as jnp
from jax import lax
from jax.experimental import pallas as pl
from jax.experimental.pallas import tpu as pltpu
from jax.sharding import PartitionSpec as P

HEADS = 4
BLOCK = 128
CORES = 2
LANES = 128
FAR = -(2.0**30)
F32 = jnp.float32
BF16 = jnp.bfloat16
MESH = pl.DeviceIdType.MESH


def dot(a, b, contract):
    return lax.dot_general(a, b, ((contract[:1], contract[1:]), ((), ())), preferred_element_type=F32)


def kernel(
    chips, depth,
    feats, table, cat, lists, count, keys, values, w_query, gain, w_up, w_down,
    out,
    feats_v, wq_v, up_v, down_v, kv, key_mix, value_mix, query_v, query_in, mask_v, mask_in,
    total, part_out, part_in, slice_out, slice_in,
    load_sem, pair_send, pair_recv, query_send, query_recv, mask_send, mask_recv,
    part_send, part_recv, slice_send, slice_recv, out_send, out_recv,
):
    rows, width = feats.shape
    head_width = width // HEADS
    tile_heads = LANES // head_width
    tiles = width // LANES
    blocks = keys.shape[0] // BLOCK
    pairs = blocks // 2
    chunk = rows // depth
    cand = lax.axis_index("cand")
    hist = lax.axis_index("hist")
    chip = cand // CORES
    core = cand % CORES
    partner = {"cand": cand + 1 - 2 * core}

    def x_peer(step):
        return {"cand": ((chip + step + chips) % chips) * CORES + core}

    def z_peer(step):
        return {"hist": (hist + step) % depth}

    barrier = pltpu.get_barrier_semaphore()
    peers = [partner] + [x_peer(j) for j in range(1, chips)] + [z_peer(k) for k in range(1, depth)]
    for peer in peers:
        pl.semaphore_signal(barrier, inc=1, device_id=peer, device_id_type=MESH)

    pieces = [(feats, feats_v), (w_query, wq_v), (keys, kv.at[0]), (values, kv.at[1]), (w_up, up_v), (w_down, down_v)]
    loads = [pltpu.make_async_copy(a, b, load_sem.at[i]) for i, (a, b) in enumerate(pieces)]
    for load in loads:
        load.start()

    def remote(src, dst, send, recv, peer):
        return pltpu.make_async_remote_copy(
            src_ref=src, dst_ref=dst, send_sem=send, recv_sem=recv, device_id=peer, device_id_type=MESH
        )

    category = cat[...]
    slots = lax.broadcasted_iota(jnp.int32, lists.shape, 0)
    live = jnp.where(slots < count[...], lists[...], -1)
    row_id = lax.broadcasted_iota(jnp.int32, (16, rows), 0)
    for j in range(chips):
        owner_chip = (chip + j) % chips
        mask = jnp.where(row_id == CORES * pairs, category.astype(F32), 0.0)
        for r in range(CORES * pairs):
            owner = owner_chip * CORES + r // pairs
            wanted = (owner * depth + hist) * blocks + 2 * (r % pairs) + category
            missing = jnp.min(jnp.where(live == wanted, 0.0, 1.0), axis=0, keepdims=True)
            mask = jnp.where(row_id == r, missing, mask)
        mask_v[j] = mask.astype(BF16)

    spread_row = lax.broadcasted_iota(jnp.int32, (16, 2 * LANES), 0)
    spread_lane = lax.broadcasted_iota(jnp.int32, (16, 2 * LANES), 1)
    spread = jnp.where(
        spread_lane < LANES,
        jnp.where((spread_lane % head_width == spread_row) & (spread_row < CORES * pairs), 1.0, 0.0),
        jnp.where(spread_row == CORES * pairs, 1.0, 0.0),
    ).astype(BF16)

    def expand(mask):
        both = dot(mask, spread, (0, 0))
        return both[:, :LANES].astype(BF16), both[:, LANES:]

    own_mask, own_second = expand(mask_v[0])

    loads[0].wait()
    loads[1].wait()
    table_f = table[...].astype(F32)
    inputs = []
    for t in range(tiles):
        cut = slice(t * LANES, (t + 1) * LANES)
        embedded = jnp.where(own_second > 0.5, table_f[1:2, cut], table_f[0:1, cut])
        inputs.append((feats_v[:, cut].astype(F32) + embedded).astype(BF16))
    scale = 0.5 / math.sqrt(head_width)
    query_v[...] = (dot(jnp.concatenate(inputs, axis=1), wq_v[...], (1, 0)) * scale).astype(BF16)

    pl.semaphore_wait(barrier, len(peers))
    query_copies, mask_copies = [], []
    for j in range(1, chips):
        query_copies.append(remote(query_v, query_in.at[j - 1], query_send.at[j - 1], query_recv.at[j - 1], x_peer(j)))
        mask_copies.append(remote(mask_v.at[j], mask_in.at[j - 1], mask_send.at[j - 1], mask_recv.at[j - 1], x_peer(j)))
        mask_copies[-1].start()
        query_copies[-1].start()
    pair_copies = [
        remote(keys, kv.at[2], pair_send.at[0], pair_recv.at[0], partner),
        remote(values, kv.at[3], pair_send.at[1], pair_recv.at[1], partner),
    ]
    for copy in pair_copies:
        copy.start()

    lane = lax.broadcasted_iota(jnp.int32, (1, LANES), 1)
    head_lane = [jnp.where(lane // head_width == a, 1.0, 0.0).astype(BF16) for a in range(tile_heads)]
    other_lane = [jnp.where(lane // head_width == a, 0.0, 1.0).astype(BF16) for a in range(tile_heads)]

    def mix_keys(side):
        owner = core if side == 0 else 1 - core
        for p in range(pairs):
            dst = slice(p * BLOCK, (p + 1) * BLOCK)
            even = slice(2 * p * BLOCK, (2 * p + 1) * BLOCK)
            odd = slice((2 * p + 1) * BLOCK, (2 * p + 2) * BLOCK)
            for t in range(tiles):
                cut = slice(t * LANES, (t + 1) * LANES)
                first, second = kv[2 * side, even, cut], kv[2 * side, odd, cut]
                for a in range(tile_heads):
                    spot = ((a + 1) % tile_heads) * head_width + owner * pairs + p
                    away = jnp.where(lane == spot, FAR, 0.0).astype(BF16)
                    key_mix[side, t * tile_heads + a, dst, :LANES] = first * head_lane[a] + away
                    key_mix[side, t * tile_heads + a, dst, LANES:] = second

    def mix_values(side):
        for p in range(pairs):
            dst = slice(p * BLOCK, (p + 1) * BLOCK)
            even = slice(2 * p * BLOCK, (2 * p + 1) * BLOCK)
            odd = slice((2 * p + 1) * BLOCK, (2 * p + 2) * BLOCK)
            for t in range(tiles):
                cut = slice(t * LANES, (t + 1) * LANES)
                value_mix[side, t, dst, :LANES] = kv[2 * side + 1, even, cut]
                value_mix[side, t, dst, LANES:] = kv[2 * side + 1, odd, cut]

    def mix_query(query_ref, mask, second):
        second_b = second.astype(BF16)
        first_b = (1.0 - second).astype(BF16)
        mixed = []
        for h in range(HEADS):
            t, a = h // tile_heads, h % tile_heads
            piece = query_ref[:, t * LANES : (t + 1) * LANES] * head_lane[a]
            mixed.append(jnp.concatenate([piece * first_b + mask * other_lane[a], piece * second_b], axis=1))
        return mixed

    def attend(mixed, second, sides):
        parts = []
        for t in range(tiles):
            picked = None
            for a in range(tile_heads):
                h = t * tile_heads + a
                acc = None
                for side in sides:
                    half = dot(mixed[h], key_mix[side, h], (1, 1))
                    weight = (half + half * jnp.tanh(half)).astype(BF16)
                    term = dot(weight, value_mix[side, t], (1, 0))
                    acc = term if acc is None else acc + term
                chosen = jnp.where(second > 0.5, acc[:, LANES:], acc[:, :LANES])
                picked = chosen if a == 0 else jnp.where(lane // head_width == a, chosen, picked)
            parts.append(picked)
        return jnp.concatenate(parts, axis=1)

    own_mixed = mix_query(query_v, own_mask, own_second)
    loads[2].wait()
    mix_keys(0)
    loads[3].wait()
    mix_values(0)
    total[...] = attend(own_mixed, own_second, (0,))
    for copy in pair_copies:
        copy.wait_recv()
    mix_keys(1)
    mix_values(1)

    part_copies = []
    for j in range(1, chips):
        mask_copies[j - 1].wait_recv()
        query_copies[j - 1].wait_recv()
        mask, second = expand(mask_in[j - 1])
        mixed = mix_query(query_in.at[j - 1], mask, second)
        part_out[j - 1] = attend(mixed, second, (0, 1)).astype(BF16)
        part_copies.append(
            remote(part_out.at[j - 1], part_in.at[j - 1], part_send.at[j - 1], part_recv.at[j - 1], x_peer(-j))
        )
        part_copies[-1].start()
    total[...] += attend(own_mixed, own_second, (1,))
    for j in range(1, chips):
        part_copies[j - 1].wait_recv()
        total[...] += part_in[j - 1].astype(F32)

    slice_out[...] = total[...].astype(BF16)
    slice_copies = []
    for k in range(1, depth):
        start = pl.multiple_of(((hist + k) % depth) * chunk, chunk)
        slice_copies.append(
            remote(slice_out.at[pl.ds(start, chunk)], slice_in.at[k - 1], slice_send.at[k - 1], slice_recv.at[k - 1], z_peer(k))
        )
        slice_copies[-1].start()
    mine = pl.ds(pl.multiple_of(hist * chunk, chunk), chunk)
    attended = total[mine, :]
    for k in range(1, depth):
        slice_copies[k - 1].wait_recv()
        attended += slice_in[k - 1].astype(F32)

    mean_square = jnp.mean(attended * attended, axis=-1, keepdims=True)
    normed = (attended * lax.rsqrt(mean_square + 1e-06) * gain[...]).astype(BF16)
    loads[4].wait()
    half = dot(normed, up_v[...], (1, 0)) * 0.5
    hidden = (half + half * jnp.tanh(half)).astype(BF16)
    loads[5].wait()
    result = feats_v[mine, :].astype(F32) + dot(hidden, down_v[...], (1, 0))
    out[mine, :] = result.astype(BF16)
    out_copies = []
    for k in range(1, depth):
        out_copies.append(remote(out.at[mine], out.at[mine], out_send.at[k - 1], out_recv.at[k - 1], z_peer(k)))
        out_copies[-1].start()
    for copy in query_copies + mask_copies + pair_copies + part_copies + slice_copies:
        copy.wait_send()
    for copy in out_copies:
        copy.wait()


def shards(chips, depth, feats, table, cat, lists, count, keys, values, w_query, gain, w_up, w_down):
    rows, width = feats.shape
    hidden = w_up.shape[1]
    history = keys.shape[0]
    chunk = rows // depth
    far, deep = max(chips - 1, 1), max(depth - 1, 1)
    vmem = pl.BlockSpec(memory_space=pltpu.VMEM)
    hbm = pl.BlockSpec(memory_space=pltpu.HBM)
    dma = pltpu.SemaphoreType.DMA
    scratch = [
        pltpu.VMEM((rows, width), BF16),
        pltpu.VMEM((width, width), BF16),
        pltpu.VMEM((width, hidden), BF16),
        pltpu.VMEM((hidden, width), BF16),
        pltpu.VMEM((4, history, width), BF16),
        pltpu.VMEM((2, HEADS, history // 2, 2 * LANES), BF16),
        pltpu.VMEM((2, width // LANES, history // 2, 2 * LANES), BF16),
        pltpu.VMEM((rows, width), BF16),
        pltpu.VMEM((far, rows, width), BF16),
        pltpu.VMEM((chips, 16, rows), BF16),
        pltpu.VMEM((far, 16, rows), BF16),
        pltpu.VMEM((rows, width), F32),
        pltpu.VMEM((far, rows, width), BF16),
        pltpu.VMEM((far, rows, width), BF16),
        pltpu.VMEM((rows, width), BF16),
        pltpu.VMEM((deep, chunk, width), BF16),
        dma((6,)), dma((2,)), dma((2,)),
        dma((far,)), dma((far,)), dma((far,)), dma((far,)), dma((far,)), dma((far,)),
        dma((deep,)), dma((deep,)), dma((deep,)), dma((deep,)),
    ]
    return pl.pallas_call(
        functools.partial(kernel, chips, depth),
        out_shape=jax.ShapeDtypeStruct((rows, width), BF16),
        in_specs=[hbm, vmem, vmem, vmem, vmem, hbm, hbm, hbm, vmem, hbm, hbm],
        out_specs=vmem,
        scratch_shapes=scratch,
        compiler_params=pltpu.CompilerParams(
            collective_id=0, has_side_effects=True, vmem_limit_bytes=48 * 1024 * 1024
        ),
    )(
        feats, table, cat.reshape(1, rows), lists.T, count.reshape(1, rows), keys, values,
        w_query, gain.reshape(1, width), w_up, w_down,
    )


def solution(mesh):
    in_specs = (
        P(("groups", "cand"), None),
        P("groups", None),
        P(("groups", "cand")),
        P(("groups", "cand"), None),
        P(("groups", "cand")),
        P(("groups", "cand", "hist"), None),
        P(("groups", "cand", "hist"), None),
        P(),
        P(),
        P(),
        P(),
    )
    out_specs = P(("groups", "cand"), None)
    body = functools.partial(shards, mesh.shape["cand"] // CORES, mesh.shape["hist"])
    return jax.shard_map(body, mesh=mesh, in_specs=in_specs, out_specs=out_specs, check_vma=False)
```

```python
import functools
import math

import jax
import jax.numpy as jnp
from jax import lax
from jax.experimental import pallas as pl
from jax.experimental.pallas import tpu as pltpu
from jax.sharding import PartitionSpec as P

HEADS = 4
BLOCK = 128
CORES = 2
LANES = 128
FAR = -(2.0**30)
F32 = jnp.float32
BF16 = jnp.bfloat16
MESH = pl.DeviceIdType.MESH


def dot(a, b, contract):
    return lax.dot_general(a, b, ((contract[:1], contract[1:]), ((), ())), preferred_element_type=F32)


def kernel(
    chips, depth,
    feats, table, cat, lists, count, keys, values, w_query, gain, w_up, w_down,
    out,
    feats_v, wq_v, up_v, down_v, kv, key_mix, value_mix, query_v, query_in, mask_v, mask_in,
    total, part_out, part_in, slice_out, slice_in,
    load_sem, pair_send, pair_recv, query_send, query_recv, mask_send, mask_recv,
    part_send, part_recv, slice_send, slice_recv, out_send, out_recv,
):
    rows, width = feats.shape
    head_width = width // HEADS
    tile_heads = LANES // head_width
    tiles = width // LANES
    blocks = keys.shape[0] // BLOCK
    pairs = blocks // 2
    chunk = rows // depth
    cand = lax.axis_index("cand")
    hist = lax.axis_index("hist")
    chip = cand // CORES
    core = cand % CORES
    partner = {"cand": cand + 1 - 2 * core}

    def x_peer(step):
        return {"cand": ((chip + step + chips) % chips) * CORES + core}

    def z_peer(step):
        return {"hist": (hist + step) % depth}

    barrier = pltpu.get_barrier_semaphore()
    peers = [partner] + [x_peer(j) for j in range(1, chips)] + [z_peer(k) for k in range(1, depth)]
    for peer in peers:
        pl.semaphore_signal(barrier, inc=1, device_id=peer, device_id_type=MESH)

    pieces = [(feats, feats_v), (w_query, wq_v), (keys, kv.at[0]), (values, kv.at[1]), (w_up, up_v), (w_down, down_v)]
    loads = [pltpu.make_async_copy(a, b, load_sem.at[i]) for i, (a, b) in enumerate(pieces)]
    for load in loads:
        load.start()

    def remote(src, dst, send, recv, peer):
        return pltpu.make_async_remote_copy(
            src_ref=src, dst_ref=dst, send_sem=send, recv_sem=recv, device_id=peer, device_id_type=MESH
        )

    category = cat[...]
    slots = lax.broadcasted_iota(jnp.int32, lists.shape, 0)
    live = jnp.where(slots < count[...], lists[...], -1)
    row_id = lax.broadcasted_iota(jnp.int32, (16, rows), 0)
    for j in range(chips):
        owner_chip = (chip + j) % chips
        mask = jnp.where(row_id == CORES * pairs, category.astype(F32), 0.0)
        for r in range(CORES * pairs):
            owner = owner_chip * CORES + r // pairs
            wanted = (owner * depth + hist) * blocks + 2 * (r % pairs) + category
            missing = jnp.min(jnp.where(live == wanted, 0.0, 1.0), axis=0, keepdims=True)
            mask = jnp.where(row_id == r, missing, mask)
        mask_v[j] = mask.astype(BF16)

    spread_row = lax.broadcasted_iota(jnp.int32, (16, 2 * LANES), 0)
    spread_lane = lax.broadcasted_iota(jnp.int32, (16, 2 * LANES), 1)
    spread = jnp.where(
        spread_lane < LANES,
        jnp.where((spread_lane % head_width == spread_row) & (spread_row < CORES * pairs), 1.0, 0.0),
        jnp.where(spread_row == CORES * pairs, 1.0, 0.0),
    ).astype(BF16)

    def expand(mask):
        both = dot(mask, spread, (0, 0))
        return both[:, :LANES].astype(BF16), both[:, LANES:]

    own_mask, own_second = expand(mask_v[0])

    loads[0].wait()
    loads[1].wait()
    table_f = table[...].astype(F32)
    inputs = []
    for t in range(tiles):
        cut = slice(t * LANES, (t + 1) * LANES)
        embedded = jnp.where(own_second > 0.5, table_f[1:2, cut], table_f[0:1, cut])
        inputs.append((feats_v[:, cut].astype(F32) + embedded).astype(BF16))
    scale = 0.5 / math.sqrt(head_width)
    query_v[...] = (dot(jnp.concatenate(inputs, axis=1), wq_v[...], (1, 0)) * scale).astype(BF16)

    pl.semaphore_wait(barrier, len(peers))
    query_copies, mask_copies = [], []
    for j in range(1, chips):
        query_copies.append(remote(query_v, query_in.at[j - 1], query_send.at[j - 1], query_recv.at[j - 1], x_peer(j)))
        mask_copies.append(remote(mask_v.at[j], mask_in.at[j - 1], mask_send.at[j - 1], mask_recv.at[j - 1], x_peer(j)))
        mask_copies[-1].start()
        query_copies[-1].start()
    pair_copies = [
        remote(keys, kv.at[2], pair_send.at[0], pair_recv.at[0], partner),
        remote(values, kv.at[3], pair_send.at[1], pair_recv.at[1], partner),
    ]
    for copy in pair_copies:
        copy.start()

    lane = lax.broadcasted_iota(jnp.int32, (1, LANES), 1)
    head_lane = [jnp.where(lane // head_width == a, 1.0, 0.0).astype(BF16) for a in range(tile_heads)]
    other_lane = [jnp.where(lane // head_width == a, 0.0, 1.0).astype(BF16) for a in range(tile_heads)]

    def mix_keys(side):
        owner = core if side == 0 else 1 - core
        for p in range(pairs):
            dst = slice(p * BLOCK, (p + 1) * BLOCK)
            even = slice(2 * p * BLOCK, (2 * p + 1) * BLOCK)
            odd = slice((2 * p + 1) * BLOCK, (2 * p + 2) * BLOCK)
            for t in range(tiles):
                cut = slice(t * LANES, (t + 1) * LANES)
                first, second = kv[2 * side, even, cut], kv[2 * side, odd, cut]
                for a in range(tile_heads):
                    spot = ((a + 1) % tile_heads) * head_width + owner * pairs + p
                    away = jnp.where(lane == spot, FAR, 0.0).astype(BF16)
                    key_mix[side, t * tile_heads + a, dst, :LANES] = first * head_lane[a] + away
                    key_mix[side, t * tile_heads + a, dst, LANES:] = second

    def mix_values(side):
        for p in range(pairs):
            dst = slice(p * BLOCK, (p + 1) * BLOCK)
            even = slice(2 * p * BLOCK, (2 * p + 1) * BLOCK)
            odd = slice((2 * p + 1) * BLOCK, (2 * p + 2) * BLOCK)
            for t in range(tiles):
                cut = slice(t * LANES, (t + 1) * LANES)
                value_mix[side, t, dst, :LANES] = kv[2 * side + 1, even, cut]
                value_mix[side, t, dst, LANES:] = kv[2 * side + 1, odd, cut]

    def mix_query(query_ref, mask, second):
        second_b = second.astype(BF16)
        first_b = (1.0 - second).astype(BF16)
        mixed = []
        for h in range(HEADS):
            t, a = h // tile_heads, h % tile_heads
            piece = query_ref[:, t * LANES : (t + 1) * LANES] * head_lane[a]
            mixed.append(jnp.concatenate([piece * first_b + mask * other_lane[a], piece * second_b], axis=1))
        return mixed

    def attend(mixed, second, sides):
        parts = []
        for t in range(tiles):
            picked = None
            for a in range(tile_heads):
                h = t * tile_heads + a
                acc = None
                for side in sides:
                    half = dot(mixed[h], key_mix[side, h], (1, 1))
                    weight = (half + half * jnp.tanh(half)).astype(BF16)
                    term = dot(weight, value_mix[side, t], (1, 0))
                    acc = term if acc is None else acc + term
                chosen = jnp.where(second > 0.5, acc[:, LANES:], acc[:, :LANES])
                picked = chosen if a == 0 else jnp.where(lane // head_width == a, chosen, picked)
            parts.append(picked)
        return jnp.concatenate(parts, axis=1)

    own_mixed = mix_query(query_v, own_mask, own_second)
    loads[2].wait()
    mix_keys(0)
    loads[3].wait()
    mix_values(0)
    total[...] = attend(own_mixed, own_second, (0,))
    for copy in pair_copies:
        copy.wait_recv()
    mix_keys(1)
    mix_values(1)

    part_copies = []
    for j in range(1, chips):
        mask_copies[j - 1].wait_recv()
        query_copies[j - 1].wait_recv()
        mask, second = expand(mask_in[j - 1])
        mixed = mix_query(query_in.at[j - 1], mask, second)
        part_out[j - 1] = attend(mixed, second, (0, 1)).astype(BF16)
        part_copies.append(
            remote(part_out.at[j - 1], part_in.at[j - 1], part_send.at[j - 1], part_recv.at[j - 1], x_peer(-j))
        )
        part_copies[-1].start()
    total[...] += attend(own_mixed, own_second, (1,))
    for j in range(1, chips):
        part_copies[j - 1].wait_recv()
        total[...] += part_in[j - 1].astype(F32)

    slice_out[...] = total[...].astype(BF16)
    slice_copies = []
    for k in range(1, depth):
        start = pl.multiple_of(((hist + k) % depth) * chunk, chunk)
        slice_copies.append(
            remote(slice_out.at[pl.ds(start, chunk)], slice_in.at[k - 1], slice_send.at[k - 1], slice_recv.at[k - 1], z_peer(k))
        )
        slice_copies[-1].start()
    mine = pl.ds(pl.multiple_of(hist * chunk, chunk), chunk)
    attended = total[mine, :]
    for k in range(1, depth):
        slice_copies[k - 1].wait_recv()
        attended += slice_in[k - 1].astype(F32)

    mean_square = jnp.mean(attended * attended, axis=-1, keepdims=True)
    normed = (attended * lax.rsqrt(mean_square + 1e-06) * gain[...]).astype(BF16)
    loads[4].wait()
    half = dot(normed, up_v[...], (1, 0)) * 0.5
    hidden = (half + half * jnp.tanh(half)).astype(BF16)
    loads[5].wait()
    result = feats_v[mine, :].astype(F32) + dot(hidden, down_v[...], (1, 0))
    out[mine, :] = result.astype(BF16)
    out_copies = []
    for k in range(1, depth):
        out_copies.append(remote(out.at[mine], out.at[mine], out_send.at[k - 1], out_recv.at[k - 1], z_peer(k)))
        out_copies[-1].start()
    for copy in query_copies + mask_copies + pair_copies + part_copies + slice_copies:
        copy.wait_send()
    for copy in out_copies:
        copy.wait()


def shards(chips, depth, feats, table, cat, lists, count, keys, values, w_query, gain, w_up, w_down):
    rows, width = feats.shape
    hidden = w_up.shape[1]
    history = keys.shape[0]
    chunk = rows // depth
    far, deep = max(chips - 1, 1), max(depth - 1, 1)
    vmem = pl.BlockSpec(memory_space=pltpu.VMEM)
    hbm = pl.BlockSpec(memory_space=pltpu.HBM)
    dma = pltpu.SemaphoreType.DMA
    scratch = [
        pltpu.VMEM((rows, width), BF16),
        pltpu.VMEM((width, width), BF16),
        pltpu.VMEM((width, hidden), BF16),
        pltpu.VMEM((hidden, width), BF16),
        pltpu.VMEM((4, history, width), BF16),
        pltpu.VMEM((2, HEADS, history // 2, 2 * LANES), BF16),
        pltpu.VMEM((2, width // LANES, history // 2, 2 * LANES), BF16),
        pltpu.VMEM((rows, width), BF16),
        pltpu.VMEM((far, rows, width), BF16),
        pltpu.VMEM((chips, 16, rows), BF16),
        pltpu.VMEM((far, 16, rows), BF16),
        pltpu.VMEM((rows, width), F32),
        pltpu.VMEM((far, rows, width), BF16),
        pltpu.VMEM((far, rows, width), BF16),
        pltpu.VMEM((rows, width), BF16),
        pltpu.VMEM((deep, chunk, width), BF16),
        dma((6,)), dma((2,)), dma((2,)),
        dma((far,)), dma((far,)), dma((far,)), dma((far,)), dma((far,)), dma((far,)),
        dma((deep,)), dma((deep,)), dma((deep,)), dma((deep,)),
    ]
    return pl.pallas_call(
        functools.partial(kernel, chips, depth),
        out_shape=jax.ShapeDtypeStruct((rows, width), BF16),
        in_specs=[hbm, vmem, vmem, vmem, vmem, hbm, hbm, hbm, vmem, hbm, hbm],
        out_specs=vmem,
        scratch_shapes=scratch,
        compiler_params=pltpu.CompilerParams(
            collective_id=0, has_side_effects=True, vmem_limit_bytes=64000 * 1024
        ),
    )(
        feats, table, cat.reshape(1, rows), lists.T, count.reshape(1, rows), keys, values,
        w_query, gain.reshape(1, width), w_up, w_down,
    )


def solution(mesh):
    in_specs = (
        P(("groups", "cand"), None),
        P("groups", None),
        P(("groups", "cand")),
        P(("groups", "cand"), None),
        P(("groups", "cand")),
        P(("groups", "cand", "hist"), None),
        P(("groups", "cand", "hist"), None),
        P(),
        P(),
        P(),
        P(),
    )
    out_specs = P(("groups", "cand"), None)
    body = functools.partial(shards, mesh.shape["cand"] // CORES, mesh.shape["hist"])
    return jax.shard_map(body, mesh=mesh, in_specs=in_specs, out_specs=out_specs, check_vma=False)
```
